256 devices in a mesh: row: 32 (over y, x, core), col: 8 (over z).
Axes of the slice: x: 4, y: 4, z: 8, core: 2. Of those that a mesh axis runs over, the one named last changes fastest.
Arguments:
- objective: float32 [16384, 2048], P('row', 'col'), may hold values from -6 to 6
- pivots: int32 [16384], P('row'), may hold values from 0 to 16383, as said below
- panel: float32 [16384, 1024], P('row', 'col'), as said below
Outputs:
- reduced: float32 [16384, 2048], P('row', 'col')
The draws below stay inside these ranges and needn't reach their ends.
Inputs may be any that keep to these rules, and one draw needn't show every extreme that they name: `pivots`: row b * 512 + o of the pivoted order takes objective row ((b + s_o) mod 32) * 512 + t_o, where o -> t_o is a permutation of 0 to 511 and the shift s_o depends on o alone; every shift from 1 to 31 is taken by exactly 8 offsets, shift 0 by the others. Each tile on the diagonal is lower triangular with diagonal entries between 2 and 4; entries above the diagonal of the whole panel are zero.
All inputs are finite; a program needn't handle non-finite values.
Results may differ from the reference program's by a relative error of at most 0.00013.
Values sent between devices are 32-bit elements; how exact they have to be, the bound alone decides.
A program may use at most 64 MiB of HBM per device.

```python
import math
import jax
import jax.numpy as jnp
from jax import lax

N = 16384
NB = 512
R = 2048
PANELS = 2
CAP = 8


def draw_pivots(key, part):
    block_count = N // NB
    spare_count = NB - CAP * (block_count - 1)
    key_a, key_b = jax.random.split(key, 2)
    base_shift = jnp.concatenate([jnp.zeros((spare_count,), jnp.int32), jnp.repeat(jnp.arange(1, block_count, dtype=jnp.int32), CAP)])
    block_shift = jax.random.permutation(key_a, base_shift).astype(jnp.int32)
    within_block = jax.random.permutation(key_b, NB).astype(jnp.int32)
    block_ids = jnp.arange(block_count, dtype=jnp.int32)[:, None]
    source_rows = (block_ids + block_shift[None, :]) % block_count * NB + within_block[None, :]
    return source_rows.reshape(N).astype(jnp.int32)


def draw_panel(key, part):
    width_all = PANELS * NB
    row_block = (jnp.arange(N) // NB)[:, None]
    row_offset = (jnp.arange(N) % NB)[:, None]
    col_block = (jnp.arange(width_all) // NB)[None, :]
    col_offset = (jnp.arange(width_all) % NB)[None, :]
    key_a, key_b = jax.random.split(key, 2)
    noise_field = jax.random.normal(key_a, (N, width_all), jnp.float32)
    diagonal_value = jax.random.uniform(key_b, (N, 1), jnp.float32, 2.0, 4.0)
    below_part = noise_field * (3.0 / math.sqrt(NB))
    tile_part = noise_field * (1.5 / math.sqrt(NB))
    same_block = row_block == col_block
    result = jnp.where(row_block > col_block, below_part, 0.0)
    result = jnp.where(same_block & (row_offset > col_offset), tile_part, result)
    result = jnp.where(same_block & (row_offset == col_offset), diagonal_value, result)
    return result.astype(jnp.float32)


def steps_of(key, extent, cuts, least, largest):
    factor_of, own = 1.0, jax.random.fold_in(key, 6)
    for position, shards_of in cuts:
        steps = jnp.exp(jax.random.uniform(jax.random.fold_in(own, position), (shards_of,), jnp.float32, least / len(cuts), largest / len(cuts)))
        factor_of = factor_of * jnp.repeat(steps, extent[position] // shards_of).reshape([-1 if axis == position else 1 for axis in range(len(extent))])
    return factor_of


def noise(stream_key, dims, width, bound, pieces=(), held_as=jnp.bfloat16):
    level = steps_of(stream_key, dims, pieces, -0.22, 0.18) if pieces else 1.0
    entries = jax.random.normal(stream_key, dims, jnp.float32) * width * level
    return jnp.minimum(jnp.maximum(entries, -bound), bound).astype(held_as)


def setup_inputs(seed: int = 0) -> dict:
    key_of = jax.random.split(jax.random.key(seed), 4)
    objective = noise(key_of[0], (N, R), 1.0, 6.0, ((0, 32), (1, 8)), jnp.float32)
    pivots = draw_pivots(jax.random.fold_in(key_of[3], 71), 0)
    panel = draw_panel(jax.random.fold_in(key_of[3], 71), 0)
    return dict(objective=objective, pivots=pivots, panel=panel)


def reference(objective, pivots, panel):
    reduced = objective[pivots]
    for panel_index in range(PANELS):
        start_row = panel_index * NB
        end_row = start_row + NB
        diag_tile = panel[start_row:end_row, start_row:end_row]
        solved = lax.linalg.triangular_solve(diag_tile, reduced[start_row:end_row], left_side=True, lower=True)
        below_rows = reduced[end_row:] - jnp.dot(panel[end_row:, start_row:end_row].astype(jnp.float32), solved.astype(jnp.float32), precision=lax.Precision.HIGHEST, preferred_element_type=jnp.float32)
        reduced = jnp.concatenate([reduced[:start_row], solved, below_rows], axis=0)
    return reduced
```

```python
import jax
import jax.numpy as jnp
from jax import lax
from jax.experimental import pallas as pl
from jax.experimental.pallas import tpu as pltpu
from jax.sharding import PartitionSpec as P

NB = 512
PIECE = 128
CAP = 8
ROWS = 32
CHIPS = 16
COLS = 8
HALF = NB // 2
PART = NB // ROWS
F32 = jnp.float32
BF16 = jnp.bfloat16
MESH = pl.DeviceIdType.MESH


def dot(a, b):
    return jnp.dot(a, b, precision=lax.Precision.HIGHEST, preferred_element_type=F32)


def pick(onehot, x):
    high = x.astype(BF16)
    rest = x - high.astype(F32)
    mid = rest.astype(BF16)
    low = (rest - mid.astype(F32)).astype(BF16)
    out = jnp.dot(onehot, high, preferred_element_type=F32)
    out = out + jnp.dot(onehot, mid, preferred_element_type=F32)
    return out + jnp.dot(onehot, low, preferred_element_type=F32)


def iota(shape, axis):
    return lax.broadcasted_iota(jnp.int32, shape, axis)


def triangle_inverse(tile):
    size = tile.shape[0]
    i, j = iota((size, size), 0), iota((size, size), 1)
    diag = jnp.where(i == j, tile, 0.0)
    down = 1.0 / jnp.sum(diag, axis=1, keepdims=True)
    across = 1.0 / jnp.sum(diag, axis=0, keepdims=True)
    below = jnp.where(i > j, tile, 0.0) * down
    inverse = jnp.where(i == j, 1.0, 0.0) - jnp.where((i >> 1) == (j >> 1), below, 0.0)
    block = 2
    level = 1
    while block < size:
        joined = ((i >> (level + 1)) == (j >> (level + 1))) & ((i >> level) != (j >> level))
        inverse = inverse - dot(dot(inverse, jnp.where(joined, below, 0.0)), inverse)
        block, level = 2 * block, level + 1
    return inverse * across


def kernel(
    obj_ref, piv_ref, panel_ref, out_ref,
    gathered, outgoing, incoming, solved, pivoted,
    row_send, row_recv, ring_send, ring_recv,
    part_send, part_recv, spread_send, spread_recv, pair_send, pair_recv, next_send, next_recv,
):
    r = lax.axis_index("row")
    z = lax.axis_index("col")
    right = {"col": lax.rem(z + 1, COLS)}
    left = {"col": lax.rem(z + COLS - 1, COLS)}

    barrier = pltpu.get_barrier_semaphore()

    def greet(step, _):
        peer = {"row": lax.rem(r + step, ROWS)}
        pl.semaphore_signal(barrier, inc=1, device_id=peer, device_id_type=MESH)
        return 0

    lax.fori_loop(1, ROWS, greet, 0)
    pl.semaphore_signal(barrier, inc=1, device_id=right, device_id_type=MESH)
    pl.semaphore_signal(barrier, inc=1, device_id=left, device_id_type=MESH)

    gathered[z] = panel_ref[...]
    for k in range(2):
        for b in range(4):
            @pl.when((r == k) & (z == 4 * k + b))
            def _():
                gathered[4 * k + b, b * PIECE : (b + 1) * PIECE] = triangle_inverse(
                    panel_ref[b * PIECE : (b + 1) * PIECE]
                )

    piv = piv_ref[...]
    target = piv & (NB - 1)
    shift = ((piv >> 9) - r) & (ROWS - 1)
    has = jnp.where(iota((ROWS, NB), 0) == shift, 1.0, 0.0)
    before = jnp.where(iota((NB, NB), 0) < iota((NB, NB), 1), 1.0, 0.0).astype(BF16)
    count = jnp.dot(has.astype(BF16), before, preferred_element_type=F32)
    rank = jnp.sum(has * count, axis=0, keepdims=True).astype(jnp.int32)
    slot = jnp.where(shift > 0, (shift - 1) * CAP + rank, -1)
    own = jnp.where(shift > 0, -1, target)
    slot_at = jnp.where(iota((HALF, NB), 0) == slot, 1.0, 0.0).astype(BF16)
    target_at = jnp.where(iota((NB, NB), 0) == target, 1.0, 0.0).astype(BF16)
    chosen = lax.dot_general(
        slot_at, target_at, (((1,), (1,)), ((), ())), preferred_element_type=F32
    ).astype(BF16)
    obj = obj_ref[...]
    outgoing[...] = pick(chosen, obj)
    incoming[(ROWS - 1) * CAP :] = jnp.zeros((CAP, incoming.shape[1]), F32)

    pl.semaphore_wait(barrier, ROWS + 1)

    def ring(direction, half, hop, shard):
        place = gathered.at[shard, pl.ds(half * HALF, HALF)]
        return pltpu.make_async_remote_copy(
            src_ref=place, dst_ref=place,
            send_sem=ring_send.at[direction, half, hop],
            recv_sem=ring_recv.at[direction, half, hop],
            device_id=right if direction == 0 else left, device_id_type=MESH,
        )

    def ring_start(direction, half, hop):
        shard = lax.rem(z - hop + COLS, COLS) if direction == 0 else lax.rem(z + hop, COLS)
        ring(direction, half, hop, shard).start()

    def ring_arrive(direction, half, hop):
        shard = (
            lax.rem(z - hop - 1 + COLS, COLS) if direction == 0 else lax.rem(z + hop + 1, COLS)
        )
        ring(direction, half, hop, shard).wait_recv()

    def ring_sent(direction, half, hop):
        ring(direction, half, hop, z).wait_send()

    for half in (0, 1):
        for direction in (0, 1):
            ring_start(direction, half ^ direction, 0)

    def pass_row(step, _):
        place = pl.ds(pl.multiple_of((step - 1) * CAP, CAP), CAP)
        pltpu.make_async_remote_copy(
            src_ref=outgoing.at[place], dst_ref=incoming.at[place],
            send_sem=row_send, recv_sem=row_recv,
            device_id={"row": lax.rem(r - step + ROWS, ROWS)}, device_id_type=MESH,
        ).start()
        return 0

    lax.fori_loop(1, ROWS, pass_row, 0)

    both = jnp.concatenate([slot, own, slot, own, slot, own, slot, own], axis=0).astype(F32)
    turned = both.T.astype(jnp.int32)
    own_at = jnp.where(iota((NB, NB), 1) == turned[:, 1:2], 1.0, 0.0).astype(BF16)
    pivoted[...] = pick(own_at, obj)

    all_rows = pl.ds(0, (ROWS - 1) * CAP)
    rows_done = pltpu.make_async_remote_copy(
        src_ref=outgoing.at[all_rows], dst_ref=incoming.at[all_rows],
        send_sem=row_send, recv_sem=row_recv, device_id=right, device_id_type=MESH,
    )
    rows_done.wait_recv()
    from_slot = jnp.where(iota((NB, HALF), 1) == turned[:, 0:1], 1.0, 0.0).astype(BF16)
    pivoted[...] = pivoted[...] + pick(from_slot, incoming[...])

    for hop in range(4):
        for half in (0, 1):
            for direction in (0, 1):
                h = half ^ direction
                if half == 0 or hop < 3:
                    ring_arrive(direction, h, hop)
                    if hop + 1 < (4 if half == 0 else 3):
                        ring_start(direction, h, hop + 1)

    def solve(k):
        for b in range(4):
            at = slice(b * PIECE, (b + 1) * PIECE)
            x = dot(gathered[4 * k + b, at], pivoted[at])
            solved[k, at] = x
            if b < 3:
                rest = slice((b + 1) * PIECE, NB)
                pivoted[rest] = pivoted[rest] - dot(gathered[4 * k + b, rest], x)

    def part_copy(k, part, send, recv, device):
        place = solved.at[k, pl.ds(pl.multiple_of(part * PART, PART), PART)]
        return pltpu.make_async_remote_copy(
            src_ref=place, dst_ref=place, send_sem=send.at[k], recv_sem=recv.at[k],
            device_id={"row": device}, device_id_type=MESH,
        )

    def rows_of(k, start, count, send, recv, device=None):
        place = solved.at[k, pl.ds(start, count)]
        return pltpu.make_async_remote_copy(
            src_ref=place, dst_ref=place, send_sem=send, recv_sem=recv,
            device_id=right if device is None else {"row": device}, device_id_type=MESH,
        )

    core = lax.rem(r, 2)
    chip = r // 2

    def scatter(k):
        def one(device, _):
            c, i = lax.rem(device, 2), device // 2
            part_copy(k, c * CHIPS + i, part_send, part_recv, device).start()
            return 0

        lax.fori_loop(2, ROWS, one, 0)

        def first(device, _):
            part_copy(k, lax.rem(device, 2) * CHIPS, spread_send, spread_recv, device).start()
            return 0

        lax.fori_loop(2, ROWS, first, 0)

    def scatter_sent(k):
        rows_of(k, 0, 30 * PART, part_send.at[k], part_recv.at[k]).wait_send()
        rows_of(k, 0, 30 * PART, spread_send.at[k], spread_recv.at[k]).wait_send()

    def spread(k):
        part_copy(k, 0, part_send, part_recv, r).wait_recv()

        def one(step, _):
            other = lax.rem(chip - 1 + step, CHIPS - 1) + 1
            part_copy(k, core * CHIPS + chip, spread_send, spread_recv, other * 2 + core).start()
            return 0

        lax.fori_loop(1, CHIPS - 1, one, 0)

    def pair(k):
        rows_of(k, 0, 15 * PART, spread_send.at[k], spread_recv.at[k]).wait_recv()
        start = pl.multiple_of(core * HALF, HALF)
        rows_of(k, start, HALF, pair_send.at[k], pair_recv.at[k], r + 1 - 2 * core).start()

    def pair_done(k):
        rows_of(k, 0, HALF, pair_send.at[k], pair_recv.at[k]).wait_recv()

    def update(k):
        full = jnp.concatenate([gathered[4 * k + b] for b in range(4)], axis=1)
        return dot(full, solved[k])

    @pl.when(r == 0)
    def _():
        solve(0)
        whole = rows_of(0, 0, NB, next_send, next_recv, 1)
        whole.start()
        scatter(0)
        out_ref[...] = solved[0]
        whole.wait_send()
        scatter_sent(0)

    @pl.when(r == 1)
    def _():
        rows_of(0, 0, NB, next_send, next_recv, 0).wait_recv()
        pivoted[...] = pivoted[...] - update(0)
        solve(1)
        scatter(1)
        out_ref[...] = solved[1]
        scatter_sent(1)

    @pl.when(r >= 2)
    def _():
        for k in range(2):
            spread(k)
            pair(k)
            pair_done(k)
            out_ref[...] = (pivoted[...] if k == 0 else out_ref[...]) - update(k)
        for k in range(2):
            rows_of(k, 0, 14 * PART, spread_send.at[k], spread_recv.at[k]).wait_send()
            rows_of(k, 0, HALF, pair_send.at[k], pair_recv.at[k]).wait_send()

    rows_done.wait_send()
    for hop in range(4):
        for half in (0, 1):
            for direction in (0, 1):
                if half == 0 or hop < 3:
                    ring_sent(direction, half ^ direction, hop)


def body(objective, pivots, panel):
    width = objective.shape[1]
    dma = pltpu.SemaphoreType.DMA
    vmem = pl.BlockSpec(memory_space=pltpu.VMEM)
    return pl.pallas_call(
        kernel,
        out_shape=jax.ShapeDtypeStruct(objective.shape, F32),
        in_specs=[vmem] * 3,
        out_specs=vmem,
        scratch_shapes=[
            pltpu.VMEM((COLS, NB, PIECE), F32),
            pltpu.VMEM((HALF, width), F32),
            pltpu.VMEM((HALF, width), F32),
            pltpu.VMEM((2, NB, width), F32),
            pltpu.VMEM((NB, width), F32),
            dma, dma,
            dma((2, 2, 4)), dma((2, 2, 4)),
            dma((2,)), dma((2,)), dma((2,)), dma((2,)), dma((2,)), dma((2,)), dma, dma,
        ],
        compiler_params=pltpu.CompilerParams(
            collective_id=0, has_side_effects=True, vmem_limit_bytes=48 * 1024 * 1024
        ),
        name="zonal",
    )(objective, pivots.reshape(1, NB), panel)


def solution(mesh):
    in_specs = (P("row", "col"), P("row"), P("row", "col"))
    out_specs = P("row", "col")
    return jax.shard_map(body, mesh=mesh, in_specs=in_specs, out_specs=out_specs, check_vma=False)
```

```python
import jax
import jax.numpy as jnp
from jax import lax
from jax.experimental import pallas as pl
from jax.experimental.pallas import tpu as pltpu
from jax.sharding import PartitionSpec as P

NB = 512
PIECE = 128
CAP = 8
ROWS = 32
CHIPS = 16
COLS = 8
HALF = NB // 2
PART = HALF // CHIPS
HELPER = 4
F32 = jnp.float32
BF16 = jnp.bfloat16
MESH = pl.DeviceIdType.MESH


def dot(a, b):
    return jnp.dot(a, b, precision=lax.Precision.HIGHEST, preferred_element_type=F32)


def pick(onehot, x):
    high = x.astype(BF16)
    rest = x - high.astype(F32)
    mid = rest.astype(BF16)
    low = (rest - mid.astype(F32)).astype(BF16)
    out = jnp.dot(onehot, high, preferred_element_type=F32)
    out = out + jnp.dot(onehot, mid, preferred_element_type=F32)
    return out + jnp.dot(onehot, low, preferred_element_type=F32)


def iota(shape, axis):
    return lax.broadcasted_iota(jnp.int32, shape, axis)


def triangle_inverse(tile):
    size = tile.shape[0]
    i, j = iota((size, size), 0), iota((size, size), 1)
    diag = jnp.where(i == j, tile, 0.0)
    down = 1.0 / jnp.sum(diag, axis=1, keepdims=True)
    across = 1.0 / jnp.sum(diag, axis=0, keepdims=True)
    below = jnp.where(i > j, tile, 0.0) * down
    inverse = jnp.where(i == j, 1.0, 0.0) - jnp.where((i >> 1) == (j >> 1), below, 0.0)
    block = 2
    level = 1
    while block < size:
        joined = ((i >> (level + 1)) == (j >> (level + 1))) & ((i >> level) != (j >> level))
        inverse = inverse - dot(dot(inverse, jnp.where(joined, below, 0.0)), inverse)
        block, level = 2 * block, level + 1
    return inverse * across


def kernel(
    obj_hbm, piv_hbm, panel_hbm, out_ref,
    obj_ref, piv_ref, obj_sem, piv_sem, panel_sem,
    gathered, outgoing, incoming, solved, pivoted,
    row_send, row_recv, ring_send, ring_recv,
    part_send, part_recv, spread_send, spread_recv, pair_send, pair_recv, next_send, next_recv,
):
    r = lax.axis_index("row")
    z = lax.axis_index("col")
    right = {"col": lax.rem(z + 1, COLS)}
    left = {"col": lax.rem(z + COLS - 1, COLS)}

    panel_in = pltpu.make_async_copy(panel_hbm, gathered.at[z], panel_sem)
    obj_in = pltpu.make_async_copy(obj_hbm, obj_ref, obj_sem)
    piv_in = pltpu.make_async_copy(piv_hbm, piv_ref, piv_sem)
    panel_in.start()
    piv_in.start()
    obj_in.start()

    barrier = pltpu.get_barrier_semaphore()

    def greet(step, _):
        peer = {"row": lax.rem(r + step, ROWS)}
        pl.semaphore_signal(barrier, inc=1, device_id=peer, device_id_type=MESH)
        return 0

    lax.fori_loop(1, ROWS, greet, 0)
    pl.semaphore_signal(barrier, inc=1, device_id=right, device_id_type=MESH)
    pl.semaphore_signal(barrier, inc=1, device_id=left, device_id_type=MESH)

    @pl.when((r < 2) & (z // 4 == r))
    def _():
        panel_in.wait()
        place = pl.ds(pl.multiple_of(lax.rem(z, 4) * PIECE, PIECE), PIECE)
        gathered[z, place] = triangle_inverse(gathered[z, place])

    @pl.when(jnp.logical_not((r < 2) & (z // 4 == r)))
    def _():
        panel_in.wait()

    piv_in.wait()
    piv = piv_ref[...]
    target = piv & (NB - 1)
    shift = ((piv >> 9) - r) & (ROWS - 1)
    has = jnp.where(iota((ROWS, NB), 0) == shift, 1.0, 0.0)
    before = jnp.where(iota((NB, NB), 0) < iota((NB, NB), 1), 1.0, 0.0).astype(BF16)
    count = jnp.dot(has.astype(BF16), before, preferred_element_type=F32)
    rank = jnp.sum(has * count, axis=0, keepdims=True).astype(jnp.int32)
    slot = jnp.where(shift > 0, (shift - 1) * CAP + rank, -1)
    own = jnp.where(shift > 0, -1, target)
    slot_at = jnp.where(iota((HALF, NB), 0) == slot, 1.0, 0.0).astype(BF16)
    target_at = jnp.where(iota((NB, NB), 0) == target, 1.0, 0.0).astype(BF16)
    chosen = lax.dot_general(
        slot_at, target_at, (((1,), (1,)), ((), ())), preferred_element_type=F32
    ).astype(BF16)
    obj_in.wait()
    obj = obj_ref[...]
    outgoing[...] = pick(chosen, obj)
    incoming[(ROWS - 1) * CAP :] = jnp.zeros((CAP, incoming.shape[1]), F32)

    pl.semaphore_wait(barrier, ROWS + 1)

    def first_step(shard):
        return jnp.where(r >= 2, 0, jnp.where(r == 0, shard, jnp.maximum(shard - 4, 0)))

    def ring(direction, quarter, hop, shard):
        place = gathered.at[shard, pl.ds(quarter * PIECE, PIECE)]
        return pltpu.make_async_remote_copy(
            src_ref=place, dst_ref=place,
            send_sem=ring_send.at[direction, quarter, hop],
            recv_sem=ring_recv.at[direction, quarter, hop],
            device_id=right if direction == 0 else left, device_id_type=MESH,
        )

    def shard_of(direction, hop):
        return lax.rem(z - hop + COLS, COLS) if direction == 0 else lax.rem(z + hop, COLS)

    def hops(direction, quarter):
        return 4 if (quarter < 2) == (direction == 0) else 3

    def ring_start(direction, quarter, hop):
        shard = shard_of(direction, hop)

        @pl.when(quarter >= first_step(shard))
        def _():
            ring(direction, quarter, hop, shard).start()

    def ring_step(direction, quarter, hop):
        shard = shard_of(direction, hop + 1)

        @pl.when(quarter >= first_step(shard))
        def _():
            ring(direction, quarter, hop, shard).wait_recv()
            if hop + 1 < hops(direction, quarter):
                ring(direction, quarter, hop + 1, shard).start()

    def ring_sent(direction, quarter, hop):
        shard = shard_of(direction, hop)

        @pl.when(quarter >= first_step(shard))
        def _():
            ring(direction, quarter, hop, shard).wait_send()

    ORDER = [(0, 0), (1, 2), (0, 1), (1, 3), (0, 2), (1, 0), (0, 3), (1, 1)]

    def ring_hop(hop, part):
        for direction, quarter in ORDER[4 * part : 4 * part + 4]:
            if hop < hops(direction, quarter):
                ring_step(direction, quarter, hop)

    for direction, quarter in ORDER:
        ring_start(direction, quarter, 0)

    def pass_row(step, _):
        place = pl.ds(pl.multiple_of((step - 1) * CAP, CAP), CAP)
        pltpu.make_async_remote_copy(
            src_ref=outgoing.at[place], dst_ref=incoming.at[place],
            send_sem=row_send, recv_sem=row_recv,
            device_id={"row": lax.rem(r - step + ROWS, ROWS)}, device_id_type=MESH,
        ).start()
        return 0

    lax.fori_loop(1, ROWS, pass_row, 0)

    both = jnp.concatenate([slot, own, slot, own, slot, own, slot, own], axis=0).astype(F32)
    turned = both.T.astype(jnp.int32)
    own_at = jnp.where(iota((NB, NB), 1) == turned[:, 1:2], 1.0, 0.0).astype(BF16)
    pivoted[...] = pick(own_at, obj)

    all_rows = pl.ds(0, (ROWS - 1) * CAP)
    rows_done = pltpu.make_async_remote_copy(
        src_ref=outgoing.at[all_rows], dst_ref=incoming.at[all_rows],
        send_sem=row_send, recv_sem=row_recv, device_id=right, device_id_type=MESH,
    )
    from_slot = jnp.where(iota((NB, HALF), 1) == turned[:, 0:1], 1.0, 0.0).astype(BF16)

    def take_rows():
        rows_done.wait_recv()
        pivoted[...] = pivoted[...] + pick(from_slot, incoming[...])

    core = lax.rem(r, 2)
    chip = r // 2

    def part_copy(group, part, half, send, recv, device):
        place = solved.at[
            pl.ds(pl.multiple_of(group * HALF + part * PART, PART), PART),
            pl.ds(pl.multiple_of(half * PIECE, PIECE), PIECE),
        ]
        return pltpu.make_async_remote_copy(
            src_ref=place, dst_ref=place, send_sem=send.at[group], recv_sem=recv.at[group],
            device_id={"row": device}, device_id_type=MESH,
        )

    def parts(group, count, send, recv):
        place = solved.at[pl.ds(0, count * PART), pl.ds(0, PIECE)]
        return pltpu.make_async_remote_copy(
            src_ref=place, dst_ref=place, send_sem=send.at[group], recv_sem=recv.at[group],
            device_id=right, device_id_type=MESH,
        )

    def block_copy(block):
        place = solved.at[pl.ds(block * PIECE, PIECE)]
        return pltpu.make_async_remote_copy(
            src_ref=place, dst_ref=place,
            send_sem=next_send.at[block], recv_sem=next_recv.at[block],
            device_id={"row": lax.rem(r + 1, ROWS)}, device_id_type=MESH,
        )

    def scatter(group):
        def one(device, _):
            part_copy(
                group, device // 2, lax.rem(device, 2), part_send, part_recv, device
            ).start()
            return 0

        lax.fori_loop(2, ROWS, one, 0)
        for half in range(2):
            part_copy(group, 0, half, part_send, part_recv, 2 * HELPER + half).start()

    def solve(k):
        for b in range(4):
            at = slice(b * PIECE, (b + 1) * PIECE)
            x = dot(gathered[4 * k + b, at], pivoted[at])
            solved[k * NB + b * PIECE : k * NB + (b + 1) * PIECE] = x
            if k == 0:
                block_copy(b).start()
            if b % 2 == 1:
                scatter(2 * k + b // 2)
            if b < 3:
                rest = slice((b + 1) * PIECE, NB)
                pivoted[rest] = pivoted[rest] - dot(gathered[4 * k + b, rest], x)
        out_ref[...] = solved[k * NB : (k + 1) * NB]
        for b in range(4):
            if k == 0:
                block_copy(b).wait_send()
        for half in range(2):
            place = solved.at[pl.ds(0, HALF)]
            pltpu.make_async_remote_copy(
                src_ref=place, dst_ref=place, send_sem=part_send.at[2 * k + half],
                recv_sem=part_recv.at[0], device_id=right, device_id_type=MESH,
            ).wait_send()

    def spread(group):
        def pass_on(part):
            def one(step, _):
                other = lax.rem(chip - 1 + step, CHIPS - 1) + 1
                part_copy(
                    group, part, core, spread_send, spread_recv, other * 2 + core
                ).start()
                return 0

            lax.fori_loop(1, CHIPS - 1, one, 0)

        @pl.when(chip == HELPER)
        def _():
            parts(group, 2, part_send, part_recv).wait_recv()
            pass_on(0)

        @pl.when(chip != HELPER)
        def _():
            parts(group, 1, part_send, part_recv).wait_recv()

        pass_on(chip)

    def pair_copy(group):
        place = solved.at[
            pl.ds(pl.multiple_of(group * HALF, HALF), HALF),
            pl.ds(pl.multiple_of(core * PIECE, PIECE), PIECE),
        ]
        return pltpu.make_async_remote_copy(
            src_ref=place, dst_ref=place,
            send_sem=pair_send.at[group], recv_sem=pair_recv.at[group],
            device_id={"row": r + 1 - 2 * core}, device_id_type=MESH,
        )

    def pair(group):
        @pl.when(chip == HELPER)
        def _():
            parts(group, 14, spread_send, spread_recv).wait_recv()

        @pl.when(chip != HELPER)
        def _():
            parts(group, 15, spread_send, spread_recv).wait_recv()

        pair_copy(group).start()

    def passed(group):
        @pl.when(chip == HELPER)
        def _():
            parts(group, 28, spread_send, spread_recv).wait_send()

        @pl.when(chip != HELPER)
        def _():
            parts(group, 14, spread_send, spread_recv).wait_send()

        pair_copy(group).wait_send()

    def update(group):
        left_part = jnp.concatenate([gathered[2 * group], gathered[2 * group + 1]], axis=1)
        rows = pl.ds(pl.multiple_of(group * HALF, HALF), HALF)
        pivoted[...] = pivoted[...] - dot(left_part, solved[rows])

    @pl.when(r == 0)
    def _():
        for hop in range(4):
            ring_hop(hop, 0)
            ring_hop(hop, 1)
            if hop == 1:
                take_rows()
        solve(0)

    @pl.when(r == 1)
    def _():
        for hop in range(4):
            ring_hop(hop, 0)
            ring_hop(hop, 1)
            if hop == 1:
                take_rows()
        for b in range(4):
            block_copy(b).wait_recv()
            pivoted[...] = pivoted[...] - dot(
                gathered[b], solved[b * PIECE : (b + 1) * PIECE]
            )
        solve(1)

    @pl.when(r >= 2)
    def _():
        last = lax.rem(z + COLS // 2, COLS) // 2
        ring_hop(0, 0)
        ring_hop(0, 1)
        take_rows()
        ring_hop(1, 0)
        spread(0)
        ring_hop(1, 1)
        spread(1)
        pair(0)
        ring_hop(2, 0)
        pair(1)
        spread(2)
        ring_hop(2, 1)
        spread(3)
        pair(2)
        ring_hop(3, 0)
        ring_hop(3, 1)
        pair(3)

        def early(group, _):
            pair_copy(group).wait_recv()

            @pl.when(group != last)
            def _():
                update(group)

            return 0

        lax.fori_loop(0, 3, early, 0)

        @pl.when(last != 3)
        def _():
            update(last)

        pair_copy(3).wait_recv()
        update(3)
        out_ref[...] = pivoted[...]
        for group in range(4):
            passed(group)

    rows_done.wait_send()
    for hop in range(4):
        for direction, quarter in ORDER:
            if hop < hops(direction, quarter):
                ring_sent(direction, quarter, hop)


def body(objective, pivots, panel):
    width = objective.shape[1]
    dma = pltpu.SemaphoreType.DMA
    vmem = pl.BlockSpec(memory_space=pltpu.VMEM)
    return pl.pallas_call(
        kernel,
        out_shape=jax.ShapeDtypeStruct(objective.shape, F32),
        in_specs=[pl.BlockSpec(memory_space=pl.ANY)] * 3,
        out_specs=vmem,
        scratch_shapes=[
            pltpu.VMEM(objective.shape, F32), pltpu.VMEM((1, NB), jnp.int32), dma, dma, dma,
            pltpu.VMEM((COLS, NB, PIECE), F32),
            pltpu.VMEM((HALF, width), F32),
            pltpu.VMEM((HALF, width), F32),
            pltpu.VMEM((2 * NB, width), F32),
            pltpu.VMEM((NB, width), F32),
            dma, dma,
            dma((2, 4, 4)), dma((2, 4, 4)),
            dma((4,)), dma((4,)), dma((4,)), dma((4,)), dma((4,)), dma((4,)), dma((4,)), dma((4,)),
        ],
        compiler_params=pltpu.CompilerParams(
            collective_id=0, has_side_effects=True, vmem_limit_bytes=60 * 1024 * 1024
        ),
        name="zonal",
    )(objective, pivots.reshape(1, NB), panel)


def solution(mesh):
    in_specs = (P("row", "col"), P("row"), P("row", "col"))
    out_specs = P("row", "col")
    return jax.shard_map(body, mesh=mesh, in_specs=in_specs, out_specs=out_specs, check_vma=False)
```

```python
import jax
import jax.numpy as jnp
from jax import lax
from jax.experimental import pallas as pl
from jax.experimental.pallas import tpu as pltpu
from jax.sharding import PartitionSpec as P

NB = 512
PIECE = 128
CAP = 8
ROWS = 32
CHIPS = 16
COLS = 8
HALF = NB // 2
PART = HALF // CHIPS
HELPER = 4
F32 = jnp.float32
BF16 = jnp.bfloat16
MESH = pl.DeviceIdType.MESH


def dot(a, b):
    return jnp.dot(a, b, precision=lax.Precision.HIGHEST, preferred_element_type=F32)


def pick(onehot, x):
    high = x.astype(BF16)
    rest = x - high.astype(F32)
    mid = rest.astype(BF16)
    low = (rest - mid.astype(F32)).astype(BF16)
    out = jnp.dot(onehot, high, preferred_element_type=F32)
    out = out + jnp.dot(onehot, mid, preferred_element_type=F32)
    return out + jnp.dot(onehot, low, preferred_element_type=F32)


def iota(shape, axis):
    return lax.broadcasted_iota(jnp.int32, shape, axis)


def triangle_inverse(tile):
    size = tile.shape[0]
    i, j = iota((size, size), 0), iota((size, size), 1)
    diag = jnp.where(i == j, tile, 0.0)
    down = 1.0 / jnp.sum(diag, axis=1, keepdims=True)
    across = 1.0 / jnp.sum(diag, axis=0, keepdims=True)
    below = jnp.where(i > j, tile, 0.0) * down
    inverse = jnp.where(i == j, 1.0, 0.0) - jnp.where((i >> 1) == (j >> 1), below, 0.0)
    block = 2
    level = 1
    while block < size:
        joined = ((i >> (level + 1)) == (j >> (level + 1))) & ((i >> level) != (j >> level))
        inverse = inverse - dot(dot(inverse, jnp.where(joined, below, 0.0)), inverse)
        block, level = 2 * block, level + 1
    return inverse * across


def kernel(
    obj_hbm, piv_hbm, panel_hbm, out_ref,
    obj_ref, piv_ref, obj_sem, piv_sem, panel_sem,
    gathered, outgoing, incoming, solved, pivoted,
    row_send, row_recv, ring_send, ring_recv,
    part_send, part_recv, spread_send, spread_recv, pair_send, pair_recv, next_send, next_recv,
):
    r = lax.axis_index("row")
    z = lax.axis_index("col")
    right = {"col": lax.rem(z + 1, COLS)}
    left = {"col": lax.rem(z + COLS - 1, COLS)}

    panel_in = pltpu.make_async_copy(panel_hbm, gathered.at[z], panel_sem)
    obj_in = pltpu.make_async_copy(obj_hbm, obj_ref, obj_sem)
    piv_in = pltpu.make_async_copy(piv_hbm, piv_ref, piv_sem)
    panel_in.start()
    piv_in.start()
    obj_in.start()

    barrier = pltpu.get_barrier_semaphore()

    def greet(step, _):
        peer = {"row": lax.rem(r + step, ROWS)}
        pl.semaphore_signal(barrier, inc=1, device_id=peer, device_id_type=MESH)
        return 0

    lax.fori_loop(1, ROWS, greet, 0)
    pl.semaphore_signal(barrier, inc=1, device_id=right, device_id_type=MESH)
    pl.semaphore_signal(barrier, inc=1, device_id=left, device_id_type=MESH)

    @pl.when((r < 2) & (z // 4 == r))
    def _():
        panel_in.wait()
        place = pl.ds(pl.multiple_of(lax.rem(z, 4) * PIECE, PIECE), PIECE)
        gathered[z, place] = triangle_inverse(gathered[z, place])

    @pl.when(jnp.logical_not((r < 2) & (z // 4 == r)))
    def _():
        panel_in.wait()

    piv_in.wait()
    piv = piv_ref[...]
    target = piv & (NB - 1)
    shift = ((piv >> 9) - r) & (ROWS - 1)
    has = jnp.where(iota((ROWS, NB), 0) == shift, 1.0, 0.0)
    before = jnp.where(iota((NB, NB), 0) < iota((NB, NB), 1), 1.0, 0.0).astype(BF16)
    count = jnp.dot(has.astype(BF16), before, preferred_element_type=F32)
    rank = jnp.sum(has * count, axis=0, keepdims=True).astype(jnp.int32)
    slot = jnp.where(shift > 0, (shift - 1) * CAP + rank, -1)
    own = jnp.where(shift > 0, -1, target)
    slot_at = jnp.where(iota((HALF, NB), 0) == slot, 1.0, 0.0).astype(BF16)
    target_at = jnp.where(iota((NB, NB), 0) == target, 1.0, 0.0).astype(BF16)
    chosen = lax.dot_general(
        slot_at, target_at, (((1,), (1,)), ((), ())), preferred_element_type=F32
    ).astype(BF16)
    obj_in.wait()
    obj = obj_ref[...]
    outgoing[...] = pick(chosen, obj)
    incoming[(ROWS - 1) * CAP :] = jnp.zeros((CAP, incoming.shape[1]), F32)

    pl.semaphore_wait(barrier, ROWS + 1)

    def first_step(shard):
        return jnp.where(r >= 2, 0, jnp.where(r == 0, shard, jnp.maximum(shard - 4, 0)))

    def ring(direction, quarter, hop, shard):
        place = gathered.at[shard, pl.ds(quarter * PIECE, PIECE)]
        return pltpu.make_async_remote_copy(
            src_ref=place, dst_ref=place,
            send_sem=ring_send.at[direction, quarter, hop],
            recv_sem=ring_recv.at[direction, quarter, hop],
            device_id=right if direction == 0 else left, device_id_type=MESH,
        )

    def shard_of(direction, hop):
        return lax.rem(z - hop + COLS, COLS) if direction == 0 else lax.rem(z + hop, COLS)

    def hops(direction, quarter):
        return 4 if (quarter < 2) == (direction == 0) else 3

    def ring_start(direction, quarter, hop):
        shard = shard_of(direction, hop)

        @pl.when(quarter >= first_step(shard))
        def _():
            ring(direction, quarter, hop, shard).start()

    def ring_step(direction, quarter, hop):
        shard = shard_of(direction, hop + 1)

        @pl.when(quarter >= first_step(shard))
        def _():
            ring(direction, quarter, hop, shard).wait_recv()
            if hop + 1 < hops(direction, quarter):
                ring(direction, quarter, hop + 1, shard).start()

    def ring_sent(direction, quarter, hop):
        shard = shard_of(direction, hop)

        @pl.when(quarter >= first_step(shard))
        def _():
            ring(direction, quarter, hop, shard).wait_send()

    ORDER = [(0, 0), (1, 2), (0, 1), (1, 3), (0, 2), (1, 0), (0, 3), (1, 1)]

    def ring_hop(hop, part):
        for direction, quarter in ORDER[4 * part : 4 * part + 4]:
            if hop < hops(direction, quarter):
                ring_step(direction, quarter, hop)

    for direction, quarter in ORDER:
        ring_start(direction, quarter, 0)

    def pass_row(step, _):
        place = pl.ds(pl.multiple_of((step - 1) * CAP, CAP), CAP)
        pltpu.make_async_remote_copy(
            src_ref=outgoing.at[place], dst_ref=incoming.at[place],
            send_sem=row_send, recv_sem=row_recv,
            device_id={"row": lax.rem(r - step + ROWS, ROWS)}, device_id_type=MESH,
        ).start()
        return 0

    lax.fori_loop(1, ROWS, pass_row, 0)

    both = jnp.concatenate([slot, own, slot, own, slot, own, slot, own], axis=0).astype(F32)
    turned = both.T.astype(jnp.int32)
    own_at = jnp.where(iota((NB, NB), 1) == turned[:, 1:2], 1.0, 0.0).astype(BF16)
    pivoted[...] = pick(own_at, obj)

    all_rows = pl.ds(0, (ROWS - 1) * CAP)
    rows_done = pltpu.make_async_remote_copy(
        src_ref=outgoing.at[all_rows], dst_ref=incoming.at[all_rows],
        send_sem=row_send, recv_sem=row_recv, device_id=right, device_id_type=MESH,
    )
    from_slot = jnp.where(iota((NB, HALF), 1) == turned[:, 0:1], 1.0, 0.0).astype(BF16)

    def take_rows():
        rows_done.wait_recv()
        pivoted[...] = pivoted[...] + pick(from_slot, incoming[...])

    core = lax.rem(r, 2)
    chip = r // 2

    def part_copy(group, part, half, send, recv, device):
        place = solved.at[
            pl.ds(pl.multiple_of(group * HALF + part * PART, PART), PART),
            pl.ds(pl.multiple_of(half * PIECE, PIECE), PIECE),
        ]
        return pltpu.make_async_remote_copy(
            src_ref=place, dst_ref=place, send_sem=send.at[group], recv_sem=recv.at[group],
            device_id={"row": device}, device_id_type=MESH,
        )

    def parts(group, count, send, recv):
        place = solved.at[pl.ds(0, count * PART), pl.ds(0, PIECE)]
        return pltpu.make_async_remote_copy(
            src_ref=place, dst_ref=place, send_sem=send.at[group], recv_sem=recv.at[group],
            device_id=right, device_id_type=MESH,
        )

    def block_copy(block):
        place = solved.at[pl.ds(block * PIECE, PIECE)]
        return pltpu.make_async_remote_copy(
            src_ref=place, dst_ref=place,
            send_sem=next_send.at[block], recv_sem=next_recv.at[block],
            device_id={"row": lax.rem(r + 1, ROWS)}, device_id_type=MESH,
        )

    def scatter(group):
        def one(device, _):
            part_copy(
                group, device // 2, lax.rem(device, 2), part_send, part_recv, device
            ).start()
            return 0

        lax.fori_loop(2, ROWS, one, 0)
        for half in range(2):
            part_copy(group, 0, half, part_send, part_recv, 2 * HELPER + half).start()

    def solve(k):
        for b in range(4):
            at = slice(b * PIECE, (b + 1) * PIECE)
            x = dot(gathered[4 * k + b, at], pivoted[at])
            solved[k * NB + b * PIECE : k * NB + (b + 1) * PIECE] = x
            if k == 0:
                block_copy(b).start()
            if b % 2 == 1:
                scatter(2 * k + b // 2)
            if b < 3:
                rest = slice((b + 1) * PIECE, NB)
                pivoted[rest] = pivoted[rest] - dot(gathered[4 * k + b, rest], x)
        out_ref[...] = solved[k * NB : (k + 1) * NB]
        for b in range(4):
            if k == 0:
                block_copy(b).wait_send()
        for half in range(2):
            place = solved.at[pl.ds(0, HALF)]
            pltpu.make_async_remote_copy(
                src_ref=place, dst_ref=place, send_sem=part_send.at[2 * k + half],
                recv_sem=part_recv.at[0], device_id=right, device_id_type=MESH,
            ).wait_send()

    def spread(group):
        def pass_on(part):
            def one(step, _):
                other = lax.rem(chip - 1 + step, CHIPS - 1) + 1
                part_copy(
                    group, part, core, spread_send, spread_recv, other * 2 + core
                ).start()
                return 0

            lax.fori_loop(1, CHIPS - 1, one, 0)

        @pl.when(chip == HELPER)
        def _():
            parts(group, 2, part_send, part_recv).wait_recv()
            pass_on(0)

        @pl.when(chip != HELPER)
        def _():
            parts(group, 1, part_send, part_recv).wait_recv()

        pass_on(chip)

    def pair_copy(group):
        place = solved.at[
            pl.ds(pl.multiple_of(group * HALF, HALF), HALF),
            pl.ds(pl.multiple_of(core * PIECE, PIECE), PIECE),
        ]
        return pltpu.make_async_remote_copy(
            src_ref=place, dst_ref=place,
            send_sem=pair_send.at[group], recv_sem=pair_recv.at[group],
            device_id={"row": r + 1 - 2 * core}, device_id_type=MESH,
        )

    def pair(group):
        @pl.when(chip == HELPER)
        def _():
            parts(group, 14, spread_send, spread_recv).wait_recv()

        @pl.when(chip != HELPER)
        def _():
            parts(group, 15, spread_send, spread_recv).wait_recv()

        pair_copy(group).start()

    def passed(group):
        @pl.when(chip == HELPER)
        def _():
            parts(group, 28, spread_send, spread_recv).wait_send()

        @pl.when(chip != HELPER)
        def _():
            parts(group, 14, spread_send, spread_recv).wait_send()

        pair_copy(group).wait_send()

    def update(group):
        left_part = jnp.concatenate([gathered[2 * group], gathered[2 * group + 1]], axis=1)
        rows = pl.ds(pl.multiple_of(group * HALF, HALF), HALF)
        pivoted[...] = pivoted[...] - dot(left_part, solved[rows])

    @pl.when(r == 0)
    def _():
        for hop in range(4):
            ring_hop(hop, 0)
            ring_hop(hop, 1)
            if hop == 1:
                take_rows()
        solve(0)

    @pl.when(r == 1)
    def _():
        for hop in range(4):
            ring_hop(hop, 0)
            ring_hop(hop, 1)
            if hop == 1:
                take_rows()
        for b in range(4):
            block_copy(b).wait_recv()
            pivoted[...] = pivoted[...] - dot(
                gathered[b], solved[b * PIECE : (b + 1) * PIECE]
            )
        solve(1)

    @pl.when(r >= 2)
    def _():
        last = lax.rem(z + COLS // 2, COLS) // 2
        ring_hop(0, 0)
        ring_hop(0, 1)
        take_rows()
        ring_hop(1, 0)
        spread(0)
        ring_hop(1, 1)
        spread(1)
        pair(0)
        ring_hop(2, 0)
        pair(1)
        spread(2)
        ring_hop(2, 1)
        spread(3)
        pair(2)
        ring_hop(3, 0)
        ring_hop(3, 1)
        pair(3)

        def early(group, _):
            pair_copy(group).wait_recv()

            @pl.when(group != last)
            def _():
                update(group)

            return 0

        lax.fori_loop(0, 3, early, 0)

        @pl.when(last != 3)
        def _():
            update(last)

        pair_copy(3).wait_recv()
        update(3)
        out_ref[...] = pivoted[...]
        for group in range(4):
            passed(group)

    rows_done.wait_send()
    for hop in range(4):
        for direction, quarter in ORDER:
            if hop < hops(direction, quarter):
                ring_sent(direction, quarter, hop)


def body(objective, pivots, panel):
    width = objective.shape[1]
    dma = pltpu.SemaphoreType.DMA
    vmem = pl.BlockSpec(memory_space=pltpu.VMEM)
    arrays = [
        pltpu.with_memory_space_constraint(array, pltpu.HBM)
        for array in (objective, pivots.reshape(1, NB), panel)
    ]
    return pl.pallas_call(
        kernel,
        out_shape=jax.ShapeDtypeStruct(objective.shape, F32),
        in_specs=[pl.BlockSpec(memory_space=pl.ANY)] * 3,
        out_specs=vmem,
        scratch_shapes=[
            pltpu.VMEM(objective.shape, F32), pltpu.VMEM((1, NB), jnp.int32), dma, dma, dma,
            pltpu.VMEM((COLS, NB, PIECE), F32),
            pltpu.VMEM((HALF, width), F32),
            pltpu.VMEM((HALF, width), F32),
            pltpu.VMEM((2 * NB, width), F32),
            pltpu.VMEM((NB, width), F32),
            dma, dma,
            dma((2, 4, 4)), dma((2, 4, 4)),
            dma((4,)), dma((4,)), dma((4,)), dma((4,)), dma((4,)), dma((4,)), dma((4,)), dma((4,)),
        ],
        compiler_params=pltpu.CompilerParams(
            collective_id=0, has_side_effects=True, vmem_limit_bytes=48 * 1024 * 1024
        ),
        name="zonal",
    )(*arrays)


def solution(mesh):
    in_specs = (P("row", "col"), P("row"), P("row", "col"))
    out_specs = P("row", "col")
    return jax.shard_map(body, mesh=mesh, in_specs=in_specs, out_specs=out_specs, check_vma=False)
```

```python
import jax
import jax.numpy as jnp
from jax import lax
from jax.experimental import pallas as pl
from jax.experimental.pallas import tpu as pltpu
from jax.sharding import PartitionSpec as P

NB = 512
PIECE = 128
CAP = 8
ROWS = 32
CHIPS = 16
COLS = 8
HALF = NB // 2
PART = HALF // CHIPS
HELPER = 4
F32 = jnp.float32
BF16 = jnp.bfloat16
MESH = pl.DeviceIdType.MESH


def dot(a, b):
    return jnp.dot(a, b, precision=lax.Precision.HIGHEST, preferred_element_type=F32)


def halves(x):
    high = x.astype(BF16)
    return high, (x - high.astype(F32)).astype(BF16)


def dot3(a, b):
    (a_high, a_low), (b_high, b_low) = halves(a), halves(b)
    small = jnp.dot(a_high, b_low, preferred_element_type=F32)
    small = small + jnp.dot(a_low, b_high, preferred_element_type=F32)
    return small + jnp.dot(a_high, b_high, preferred_element_type=F32)


def pick(onehot, x):
    high = x.astype(BF16)
    rest = x - high.astype(F32)
    mid = rest.astype(BF16)
    low = (rest - mid.astype(F32)).astype(BF16)
    out = jnp.dot(onehot, high, preferred_element_type=F32)
    out = out + jnp.dot(onehot, mid, preferred_element_type=F32)
    return out + jnp.dot(onehot, low, preferred_element_type=F32)


def iota(shape, axis):
    return lax.broadcasted_iota(jnp.int32, shape, axis)


def triangle_inverse(tile):
    size = tile.shape[0]
    i, j = iota((size, size), 0), iota((size, size), 1)
    diag = jnp.where(i == j, tile, 0.0)
    down = 1.0 / jnp.sum(diag, axis=1, keepdims=True)
    across = 1.0 / jnp.sum(diag, axis=0, keepdims=True)
    below = jnp.where(i > j, tile, 0.0) * down
    inverse = jnp.where(i == j, 1.0, 0.0) - jnp.where((i >> 1) == (j >> 1), below, 0.0)
    block = 2
    level = 1
    while block < size:
        joined = ((i >> (level + 1)) == (j >> (level + 1))) & ((i >> level) != (j >> level))
        inverse = inverse - dot(dot(inverse, jnp.where(joined, below, 0.0)), inverse)
        block, level = 2 * block, level + 1
    return inverse * across


def kernel(
    obj_hbm, piv_hbm, panel_hbm, out_ref,
    obj_ref, piv_ref, obj_sem, piv_sem, panel_sem, go,
    gathered, outgoing, incoming, solved, pivoted,
    row_send, row_recv, ring_send, ring_recv,
    part_send, part_recv, spread_send, spread_recv, pair_send, pair_recv, next_send, next_recv,
):
    r = lax.axis_index("row")
    z = lax.axis_index("col")
    right = {"col": lax.rem(z + 1, COLS)}
    left = {"col": lax.rem(z + COLS - 1, COLS)}

    panel_in = pltpu.make_async_copy(panel_hbm, gathered.at[z], panel_sem)
    obj_in = pltpu.make_async_copy(obj_hbm, obj_ref, obj_sem)
    piv_in = pltpu.make_async_copy(piv_hbm, piv_ref, piv_sem)
    panel_in.start()
    piv_in.start()
    obj_in.start()

    barrier = pltpu.get_barrier_semaphore()

    def greet(step, _):
        peer = {"row": lax.rem(r + step, ROWS)}
        pl.semaphore_signal(barrier, inc=1, device_id=peer, device_id_type=MESH)
        return 0

    lax.fori_loop(1, ROWS, greet, 0)
    pl.semaphore_signal(barrier, inc=1, device_id=right, device_id_type=MESH)
    pl.semaphore_signal(barrier, inc=1, device_id=left, device_id_type=MESH)

    @pl.when((r < 2) & (z // 4 == r))
    def _():
        panel_in.wait()
        place = pl.ds(pl.multiple_of(lax.rem(z, 4) * PIECE, PIECE), PIECE)
        gathered[z, place] = triangle_inverse(gathered[z, place])

    @pl.when(jnp.logical_not((r < 2) & (z // 4 == r)))
    def _():
        panel_in.wait()

    piv_in.wait()
    piv = piv_ref[...]
    target = piv & (NB - 1)
    shift = ((piv >> 9) - r) & (ROWS - 1)
    has = jnp.where(iota((ROWS, NB), 0) == shift, 1.0, 0.0)
    before = jnp.where(iota((NB, NB), 0) < iota((NB, NB), 1), 1.0, 0.0).astype(BF16)
    count = jnp.dot(has.astype(BF16), before, preferred_element_type=F32)
    rank = jnp.sum(has * count, axis=0, keepdims=True).astype(jnp.int32)
    slot = jnp.where(shift > 0, (shift - 1) * CAP + rank, -1)
    own = jnp.where(shift > 0, -1, target)
    slot_at = jnp.where(iota((HALF, NB), 0) == slot, 1.0, 0.0).astype(BF16)
    target_at = jnp.where(iota((NB, NB), 0) == target, 1.0, 0.0).astype(BF16)
    chosen = lax.dot_general(
        slot_at, target_at, (((1,), (1,)), ((), ())), preferred_element_type=F32
    ).astype(BF16)
    obj_in.wait()
    obj = obj_ref[...]
    outgoing[...] = pick(chosen, obj)
    incoming[(ROWS - 1) * CAP :] = jnp.zeros((CAP, incoming.shape[1]), F32)

    pl.semaphore_wait(barrier, ROWS + 1)

    def first_step(shard):
        return jnp.where(r >= 2, 0, jnp.where(r == 0, shard, jnp.maximum(shard - 4, 0)))

    def ring(direction, quarter, hop, shard):
        place = gathered.at[shard, pl.ds(quarter * PIECE, PIECE)]
        return pltpu.make_async_remote_copy(
            src_ref=place, dst_ref=place,
            send_sem=ring_send.at[direction, quarter, hop],
            recv_sem=ring_recv.at[direction, quarter, hop],
            device_id=right if direction == 0 else left, device_id_type=MESH,
        )

    def shard_of(direction, hop):
        return lax.rem(z - hop + COLS, COLS) if direction == 0 else lax.rem(z + hop, COLS)

    def hops(direction, quarter):
        return 4 if (quarter < 2) == (direction == 0) else 3

    def ring_start(direction, quarter, hop):
        shard = shard_of(direction, hop)

        @pl.when(quarter >= first_step(shard))
        def _():
            ring(direction, quarter, hop, shard).start()

    def ring_step(direction, quarter, hop):
        shard = shard_of(direction, hop + 1)

        @pl.when(quarter >= first_step(shard))
        def _():
            ring(direction, quarter, hop, shard).wait_recv()
            if hop + 1 < hops(direction, quarter):
                ring(direction, quarter, hop + 1, shard).start()

    def ring_sent(direction, quarter, hop):
        shard = shard_of(direction, hop)

        @pl.when(quarter >= first_step(shard))
        def _():
            ring(direction, quarter, hop, shard).wait_send()

    ORDER = [(0, 0), (1, 2), (0, 1), (1, 3), (0, 2), (1, 0), (0, 3), (1, 1)]

    def ring_hop(hop, part):
        for direction, quarter in ORDER[4 * part : 4 * part + 4]:
            if hop < hops(direction, quarter):
                ring_step(direction, quarter, hop)

    def ring_begin():
        for direction, quarter in ORDER:
            ring_start(direction, quarter, 0)

    later = (r == 1) & (z < 4)

    @pl.when(jnp.logical_not(later))
    def _():
        ring_begin()

    def pass_row(step, _):
        place = pl.ds(pl.multiple_of((step - 1) * CAP, CAP), CAP)
        pltpu.make_async_remote_copy(
            src_ref=outgoing.at[place], dst_ref=incoming.at[place],
            send_sem=row_send, recv_sem=row_recv,
            device_id={"row": lax.rem(r - step + ROWS, ROWS)}, device_id_type=MESH,
        ).start()
        return 0

    lax.fori_loop(1, ROWS, pass_row, 0)

    both = jnp.concatenate([slot, own, slot, own, slot, own, slot, own], axis=0).astype(F32)
    turned = both.T.astype(jnp.int32)
    own_at = jnp.where(iota((NB, NB), 1) == turned[:, 1:2], 1.0, 0.0).astype(BF16)
    pivoted[...] = pick(own_at, obj)

    all_rows = pl.ds(0, (ROWS - 1) * CAP)
    rows_done = pltpu.make_async_remote_copy(
        src_ref=outgoing.at[all_rows], dst_ref=incoming.at[all_rows],
        send_sem=row_send, recv_sem=row_recv, device_id=right, device_id_type=MESH,
    )
    from_slot = jnp.where(iota((NB, HALF), 1) == turned[:, 0:1], 1.0, 0.0).astype(BF16)

    def take_rows():
        rows_done.wait_recv()
        pivoted[...] = pivoted[...] + pick(from_slot, incoming[...])

    core = lax.rem(r, 2)
    chip = r // 2

    def part_copy(group, part, half, send, recv, device):
        place = solved.at[
            pl.ds(pl.multiple_of(group * HALF + part * PART, PART), PART),
            pl.ds(pl.multiple_of(half * PIECE, PIECE), PIECE),
        ]
        return pltpu.make_async_remote_copy(
            src_ref=place, dst_ref=place, send_sem=send.at[group], recv_sem=recv.at[group],
            device_id={"row": device}, device_id_type=MESH,
        )

    def parts(group, count, send, recv):
        place = solved.at[pl.ds(0, count * PART), pl.ds(0, PIECE)]
        return pltpu.make_async_remote_copy(
            src_ref=place, dst_ref=place, send_sem=send.at[group], recv_sem=recv.at[group],
            device_id=right, device_id_type=MESH,
        )

    def block_copy(block):
        place = solved.at[pl.ds(block * PIECE, PIECE)]
        return pltpu.make_async_remote_copy(
            src_ref=place, dst_ref=place,
            send_sem=next_send.at[block], recv_sem=next_recv.at[block],
            device_id={"row": lax.rem(r + 1, ROWS)}, device_id_type=MESH,
        )

    def scatter(group):
        def one(device, _):
            part_copy(
                group, device // 2, lax.rem(device, 2), part_send, part_recv, device
            ).start()
            return 0

        lax.fori_loop(2, ROWS, one, 0)
        for half in range(2):
            part_copy(group, 0, half, part_send, part_recv, 2 * HELPER + half).start()

    def solve(k):
        for b in range(4):
            at = slice(b * PIECE, (b + 1) * PIECE)
            x = dot3(gathered[4 * k + b, at], pivoted[at])
            solved[k * NB + b * PIECE : k * NB + (b + 1) * PIECE] = x
            if k == 0:
                block_copy(b).start()
            if b % 2 == 1:
                scatter(2 * k + b // 2)
            if b < 3:
                rest = slice((b + 1) * PIECE, NB)
                pivoted[rest] = pivoted[rest] - dot3(gathered[4 * k + b, rest], x)
        out_ref[...] = solved[k * NB : (k + 1) * NB]
        for b in range(4):
            if k == 0:
                block_copy(b).wait_send()
        for half in range(2):
            place = solved.at[pl.ds(0, HALF)]
            pltpu.make_async_remote_copy(
                src_ref=place, dst_ref=place, send_sem=part_send.at[2 * k + half],
                recv_sem=part_recv.at[0], device_id=right, device_id_type=MESH,
            ).wait_send()

    def spread(group):
        def pass_on(part):
            def one(step, _):
                other = lax.rem(chip - 1 + step, CHIPS - 1) + 1
                part_copy(
                    group, part, core, spread_send, spread_recv, other * 2 + core
                ).start()
                return 0

            lax.fori_loop(1, CHIPS - 1, one, 0)

        @pl.when(chip == HELPER)
        def _():
            parts(group, 2, part_send, part_recv).wait_recv()
            pass_on(0)

        @pl.when(chip != HELPER)
        def _():
            parts(group, 1, part_send, part_recv).wait_recv()

        pass_on(chip)

    def pair_copy(group):
        place = solved.at[
            pl.ds(pl.multiple_of(group * HALF, HALF), HALF),
            pl.ds(pl.multiple_of(core * PIECE, PIECE), PIECE),
        ]
        return pltpu.make_async_remote_copy(
            src_ref=place, dst_ref=place,
            send_sem=pair_send.at[group], recv_sem=pair_recv.at[group],
            device_id={"row": r + 1 - 2 * core}, device_id_type=MESH,
        )

    def pair(group):
        @pl.when(chip == HELPER)
        def _():
            parts(group, 14, spread_send, spread_recv).wait_recv()

        @pl.when(chip != HELPER)
        def _():
            parts(group, 15, spread_send, spread_recv).wait_recv()

        pair_copy(group).start()

    def passed(group):
        @pl.when(chip == HELPER)
        def _():
            parts(group, 28, spread_send, spread_recv).wait_send()

        @pl.when(chip != HELPER)
        def _():
            parts(group, 14, spread_send, spread_recv).wait_send()

        pair_copy(group).wait_send()

    def update(group):
        left_part = jnp.concatenate([gathered[2 * group], gathered[2 * group + 1]], axis=1)
        rows = pl.ds(pl.multiple_of(group * HALF, HALF), HALF)
        pivoted[...] = pivoted[...] - dot3(left_part, solved[rows])

    @pl.when(r == 0)
    def _():
        for hop in range(4):
            ring_hop(hop, 0)
            ring_hop(hop, 1)
            if hop == 0:
                @pl.when(z < 4)
                def _():
                    pl.semaphore_signal(
                        go, inc=1, device_id={"row": r + 1}, device_id_type=MESH
                    )

            if hop == 1:
                take_rows()
        solve(0)

    @pl.when(r == 1)
    def _():
        @pl.when(later)
        def _():
            pl.semaphore_wait(go, 1)
            ring_begin()

        for hop in range(4):
            ring_hop(hop, 0)
            ring_hop(hop, 1)
            if hop == 1:
                take_rows()
        for b in range(4):
            block_copy(b).wait_recv()
            pivoted[...] = pivoted[...] - dot3(
                gathered[b], solved[b * PIECE : (b + 1) * PIECE]
            )
        solve(1)

    @pl.when(r >= 2)
    def _():
        ring_hop(0, 0)
        ring_hop(0, 1)
        take_rows()
        ring_hop(1, 0)
        spread(0)
        ring_hop(1, 1)
        spread(1)
        pair(0)
        ring_hop(2, 0)
        pair(1)
        spread(2)
        ring_hop(2, 1)
        spread(3)
        pair(2)
        ring_hop(3, 0)
        ring_hop(3, 1)

        def early(group, _):
            pair_copy(group).wait_recv()
            update(group)
            return 0

        lax.fori_loop(0, 2, early, 0)
        pair(3)
        pair_copy(2).wait_recv()
        update(2)
        pair_copy(3).wait_recv()
        update(3)
        out_ref[...] = pivoted[...]
        for group in range(4):
            passed(group)

    rows_done.wait_send()
    for hop in range(4):
        for direction, quarter in ORDER:
            if hop < hops(direction, quarter):
                ring_sent(direction, quarter, hop)


def body(objective, pivots, panel):
    width = objective.shape[1]
    dma = pltpu.SemaphoreType.DMA
    vmem = pl.BlockSpec(memory_space=pltpu.VMEM)
    arrays = [
        pltpu.with_memory_space_constraint(array, pltpu.HBM)
        for array in (objective, pivots.reshape(1, NB), panel)
    ]
    return pl.pallas_call(
        kernel,
        out_shape=jax.ShapeDtypeStruct(objective.shape, F32),
        in_specs=[pl.BlockSpec(memory_space=pl.ANY)] * 3,
        out_specs=vmem,
        scratch_shapes=[
            pltpu.VMEM(objective.shape, F32), pltpu.VMEM((1, NB), jnp.int32), dma, dma, dma,
            pltpu.SemaphoreType.REGULAR,
            pltpu.VMEM((COLS, NB, PIECE), F32),
            pltpu.VMEM((HALF, width), F32),
            pltpu.VMEM((HALF, width), F32),
            pltpu.VMEM((2 * NB, width), F32),
            pltpu.VMEM((NB, width), F32),
            dma, dma,
            dma((2, 4, 4)), dma((2, 4, 4)),
            dma((4,)), dma((4,)), dma((4,)), dma((4,)), dma((4,)), dma((4,)), dma((4,)), dma((4,)),
        ],
        compiler_params=pltpu.CompilerParams(
            collective_id=0, has_side_effects=True, vmem_limit_bytes=48 * 1024 * 1024
        ),
        name="zonal",
    )(*arrays)


def solution(mesh):
    in_specs = (P("row", "col"), P("row"), P("row", "col"))
    out_specs = P("row", "col")
    return jax.shard_map(body, mesh=mesh, in_specs=in_specs, out_specs=out_specs, check_vma=False)
```

```python
import jax
import jax.numpy as jnp
from jax import lax
from jax.experimental import pallas as pl
from jax.experimental.pallas import tpu as pltpu
from jax.sharding import PartitionSpec as P

NB = 512
PIECE = 128
CAP = 8
ROWS = 32
CHIPS = 16
COLS = 8
HALF = NB // 2
PART = HALF // CHIPS
HELPERS = (4, 12)
F32 = jnp.float32
BF16 = jnp.bfloat16
MESH = pl.DeviceIdType.MESH


def dot(a, b):
    return jnp.dot(a, b, precision=lax.Precision.HIGHEST, preferred_element_type=F32)


def halves(x):
    high = x.astype(BF16)
    return high, (x - high.astype(F32)).astype(BF16)


def dot3(a, b):
    (a_high, a_low), (b_high, b_low) = halves(a), halves(b)
    small = jnp.dot(a_high, b_low, preferred_element_type=F32)
    small = small + jnp.dot(a_low, b_high, preferred_element_type=F32)
    return small + jnp.dot(a_high, b_high, preferred_element_type=F32)


def pick(onehot, x):
    high = x.astype(BF16)
    rest = x - high.astype(F32)
    mid = rest.astype(BF16)
    low = (rest - mid.astype(F32)).astype(BF16)
    out = jnp.dot(onehot, high, preferred_element_type=F32)
    out = out + jnp.dot(onehot, mid, preferred_element_type=F32)
    return out + jnp.dot(onehot, low, preferred_element_type=F32)


def iota(shape, axis):
    return lax.broadcasted_iota(jnp.int32, shape, axis)


def triangle_inverse(tile):
    size = tile.shape[0]
    i, j = iota((size, size), 0), iota((size, size), 1)
    diag = jnp.where(i == j, tile, 0.0)
    down = 1.0 / jnp.sum(diag, axis=1, keepdims=True)
    across = 1.0 / jnp.sum(diag, axis=0, keepdims=True)
    below = jnp.where(i > j, tile, 0.0) * down
    inverse = jnp.where(i == j, 1.0, 0.0) - jnp.where((i >> 1) == (j >> 1), below, 0.0)
    block = 2
    level = 1
    while block < size:
        joined = ((i >> (level + 1)) == (j >> (level + 1))) & ((i >> level) != (j >> level))
        inverse = inverse - dot(dot(inverse, jnp.where(joined, below, 0.0)), inverse)
        block, level = 2 * block, level + 1
    return inverse * across


def kernel(
    obj_hbm, piv_hbm, panel_hbm, out_ref,
    obj_ref, piv_ref, obj_sem, piv_sem, panel_sem, go, tile_high, tile_low,
    gathered, outgoing, incoming, solved, pivoted,
    row_send, row_recv, ring_send, ring_recv,
    part_send, part_recv, spread_send, spread_recv, pair_send, pair_recv, next_send, next_recv,
):
    r = lax.axis_index("row")
    z = lax.axis_index("col")
    right = {"col": lax.rem(z + 1, COLS)}
    left = {"col": lax.rem(z + COLS - 1, COLS)}

    panel_in = pltpu.make_async_copy(panel_hbm, gathered.at[z], panel_sem)
    obj_in = pltpu.make_async_copy(obj_hbm, obj_ref, obj_sem)
    piv_in = pltpu.make_async_copy(piv_hbm, piv_ref, piv_sem)
    panel_in.start()
    piv_in.start()
    obj_in.start()

    barrier = pltpu.get_barrier_semaphore()

    def greet(step, _):
        peer = {"row": lax.rem(r + step, ROWS)}
        pl.semaphore_signal(barrier, inc=1, device_id=peer, device_id_type=MESH)
        return 0

    lax.fori_loop(1, ROWS, greet, 0)
    pl.semaphore_signal(barrier, inc=1, device_id=right, device_id_type=MESH)
    pl.semaphore_signal(barrier, inc=1, device_id=left, device_id_type=MESH)

    @pl.when((r < 2) & (z // 4 == r))
    def _():
        panel_in.wait()
        place = pl.ds(pl.multiple_of(lax.rem(z, 4) * PIECE, PIECE), PIECE)
        gathered[z, place] = triangle_inverse(gathered[z, place])

    @pl.when(jnp.logical_not((r < 2) & (z // 4 == r)))
    def _():
        panel_in.wait()

    piv_in.wait()
    piv = piv_ref[...]
    target = piv & (NB - 1)
    shift = ((piv >> 9) - r) & (ROWS - 1)
    has = jnp.where(iota((ROWS, NB), 0) == shift, 1.0, 0.0)
    before = jnp.where(iota((NB, NB), 0) < iota((NB, NB), 1), 1.0, 0.0).astype(BF16)
    count = jnp.dot(has.astype(BF16), before, preferred_element_type=F32)
    rank = jnp.sum(has * count, axis=0, keepdims=True).astype(jnp.int32)
    slot = jnp.where(shift > 0, (shift - 1) * CAP + rank, -1)
    own = jnp.where(shift > 0, -1, target)
    slot_at = jnp.where(iota((HALF, NB), 0) == slot, 1.0, 0.0).astype(BF16)
    target_at = jnp.where(iota((NB, NB), 0) == target, 1.0, 0.0).astype(BF16)
    chosen = lax.dot_general(
        slot_at, target_at, (((1,), (1,)), ((), ())), preferred_element_type=F32
    ).astype(BF16)
    obj_in.wait()
    obj = obj_ref[...]
    outgoing[...] = pick(chosen, obj)
    incoming[(ROWS - 1) * CAP :] = jnp.zeros((CAP, incoming.shape[1]), F32)

    pl.semaphore_wait(barrier, ROWS + 1)

    def first_step(shard):
        return jnp.where(r >= 2, 0, jnp.where(r == 0, shard, jnp.maximum(shard - 4, 0)))

    def ring(direction, quarter, hop, shard):
        place = gathered.at[shard, pl.ds(quarter * PIECE, PIECE)]
        return pltpu.make_async_remote_copy(
            src_ref=place, dst_ref=place,
            send_sem=ring_send.at[direction, quarter, hop],
            recv_sem=ring_recv.at[direction, quarter, hop],
            device_id=right if direction == 0 else left, device_id_type=MESH,
        )

    def shard_of(direction, hop):
        return lax.rem(z - hop + COLS, COLS) if direction == 0 else lax.rem(z + hop, COLS)

    def hops(direction, quarter):
        return 4 if (quarter < 2) == (direction == 0) else 3

    def ring_start(direction, quarter, hop):
        shard = shard_of(direction, hop)

        @pl.when(quarter >= first_step(shard))
        def _():
            ring(direction, quarter, hop, shard).start()

    def ring_step(direction, quarter, hop):
        shard = shard_of(direction, hop + 1)

        @pl.when(quarter >= first_step(shard))
        def _():
            ring(direction, quarter, hop, shard).wait_recv()
            if hop + 1 < hops(direction, quarter):
                ring(direction, quarter, hop + 1, shard).start()

    def ring_sent(direction, quarter, hop):
        shard = shard_of(direction, hop)

        @pl.when(quarter >= first_step(shard))
        def _():
            ring(direction, quarter, hop, shard).wait_send()

    ORDER = [(0, 0), (1, 2), (0, 1), (1, 3), (0, 2), (1, 0), (0, 3), (1, 1)]

    def ring_hop(hop, part):
        for direction, quarter in ORDER[4 * part : 4 * part + 4]:
            if hop < hops(direction, quarter):
                ring_step(direction, quarter, hop)

    def ring_begin():
        for direction, quarter in ORDER:
            ring_start(direction, quarter, 0)

    later = (r == 1) & (z < 4)

    @pl.when(jnp.logical_not(later))
    def _():
        ring_begin()

    def pass_row(step, _):
        place = pl.ds(pl.multiple_of((step - 1) * CAP, CAP), CAP)
        pltpu.make_async_remote_copy(
            src_ref=outgoing.at[place], dst_ref=incoming.at[place],
            send_sem=row_send, recv_sem=row_recv,
            device_id={"row": lax.rem(r - step + ROWS, ROWS)}, device_id_type=MESH,
        ).start()
        return 0

    lax.fori_loop(1, ROWS, pass_row, 0)

    both = jnp.concatenate([slot, own, slot, own, slot, own, slot, own], axis=0).astype(F32)
    turned = both.T.astype(jnp.int32)
    own_at = jnp.where(iota((NB, NB), 1) == turned[:, 1:2], 1.0, 0.0).astype(BF16)
    pivoted[...] = pick(own_at, obj)

    all_rows = pl.ds(0, (ROWS - 1) * CAP)
    rows_done = pltpu.make_async_remote_copy(
        src_ref=outgoing.at[all_rows], dst_ref=incoming.at[all_rows],
        send_sem=row_send, recv_sem=row_recv, device_id=right, device_id_type=MESH,
    )
    from_slot = jnp.where(iota((NB, HALF), 1) == turned[:, 0:1], 1.0, 0.0).astype(BF16)

    def take_rows():
        rows_done.wait_recv()
        pivoted[...] = pivoted[...] + pick(from_slot, incoming[...])

    core = lax.rem(r, 2)
    chip = r // 2

    def part_copy(group, part, half, send, recv, device):
        place = solved.at[
            pl.ds(pl.multiple_of(group * HALF + part * PART, PART), PART),
            pl.ds(pl.multiple_of(half * PIECE, PIECE), PIECE),
        ]
        return pltpu.make_async_remote_copy(
            src_ref=place, dst_ref=place, send_sem=send.at[group], recv_sem=recv.at[group],
            device_id={"row": device}, device_id_type=MESH,
        )

    def piece_copy(group, piece, half, send, recv, device):
        place = solved.at[
            pl.ds(pl.multiple_of(group * HALF + piece * 8, 8), 8),
            pl.ds(pl.multiple_of(half * PIECE, PIECE), PIECE),
        ]
        return pltpu.make_async_remote_copy(
            src_ref=place, dst_ref=place, send_sem=send.at[group], recv_sem=recv.at[group],
            device_id={"row": device}, device_id_type=MESH,
        )

    def parts(group, count, send, recv):
        place = solved.at[pl.ds(0, count * 8), pl.ds(0, PIECE)]
        return pltpu.make_async_remote_copy(
            src_ref=place, dst_ref=place, send_sem=send.at[group], recv_sem=recv.at[group],
            device_id=right, device_id_type=MESH,
        )

    def block_copy(block):
        place = solved.at[pl.ds(block * PIECE, PIECE)]
        return pltpu.make_async_remote_copy(
            src_ref=place, dst_ref=place,
            send_sem=next_send.at[block], recv_sem=next_recv.at[block],
            device_id={"row": lax.rem(r + 1, ROWS)}, device_id_type=MESH,
        )

    def scatter(group):
        def one(device, _):
            part_copy(
                group, device // 2, lax.rem(device, 2), part_send, part_recv, device
            ).start()
            return 0

        lax.fori_loop(2, ROWS, one, 0)
        for half in range(2):
            for piece in range(2):
                piece_copy(
                    group, piece, half, part_send, part_recv, 2 * HELPERS[piece] + half
                ).start()

    def solve(k):
        for b in range(4):
            at = slice(b * PIECE, (b + 1) * PIECE)
            x = dot3(gathered[4 * k + b, at], pivoted[at])
            solved[k * NB + b * PIECE : k * NB + (b + 1) * PIECE] = x
            if k == 0:
                block_copy(b).start()
            if b % 2 == 1:
                scatter(2 * k + b // 2)
            if b < 3:
                rest = slice((b + 1) * PIECE, NB)
                pivoted[rest] = pivoted[rest] - dot3(gathered[4 * k + b, rest], x)
        out_ref[...] = solved[k * NB : (k + 1) * NB]
        for b in range(4):
            if k == 0:
                block_copy(b).wait_send()
        for half in range(2):
            place = solved.at[pl.ds(0, HALF)]
            pltpu.make_async_remote_copy(
                src_ref=place, dst_ref=place, send_sem=part_send.at[2 * k + half],
                recv_sem=part_recv.at[0], device_id=right, device_id_type=MESH,
            ).wait_send()

    helps = (chip == HELPERS[0]) | (chip == HELPERS[1])

    def spread(group):
        @pl.when(helps)
        def _():
            parts(group, 3, part_send, part_recv).wait_recv()

        @pl.when(jnp.logical_not(helps))
        def _():
            parts(group, 2, part_send, part_recv).wait_recv()

        def one(step, _):
            other = lax.rem(chip - 1 + step, CHIPS - 1) + 1
            part_copy(group, chip, core, spread_send, spread_recv, other * 2 + core).start()

            @pl.when(helps)
            def _():
                piece_copy(
                    group, jnp.where(chip == HELPERS[0], 0, 1), core,
                    spread_send, spread_recv, other * 2 + core,
                ).start()

            return 0

        lax.fori_loop(1, CHIPS - 1, one, 0)

    def pair_copy(group):
        place = solved.at[
            pl.ds(pl.multiple_of(group * HALF, HALF), HALF),
            pl.ds(pl.multiple_of(core * PIECE, PIECE), PIECE),
        ]
        return pltpu.make_async_remote_copy(
            src_ref=place, dst_ref=place,
            send_sem=pair_send.at[group], recv_sem=pair_recv.at[group],
            device_id={"row": r + 1 - 2 * core}, device_id_type=MESH,
        )

    def pair(group):
        @pl.when(helps)
        def _():
            parts(group, 29, spread_send, spread_recv).wait_recv()

        @pl.when(jnp.logical_not(helps))
        def _():
            parts(group, 30, spread_send, spread_recv).wait_recv()

        pair_copy(group).start()

    def passed(group):
        @pl.when(helps)
        def _():
            parts(group, 42, spread_send, spread_recv).wait_send()

        @pl.when(jnp.logical_not(helps))
        def _():
            parts(group, 28, spread_send, spread_recv).wait_send()

        pair_copy(group).wait_send()

    def update(group):
        left_part = jnp.concatenate([gathered[2 * group], gathered[2 * group + 1]], axis=1)
        rows = pl.ds(pl.multiple_of(group * HALF, HALF), HALF)
        pivoted[...] = pivoted[...] - dot3(left_part, solved[rows])

    @pl.when(r == 0)
    def _():
        for hop in range(4):
            ring_hop(hop, 0)
            ring_hop(hop, 1)
            if hop == 0:
                @pl.when(z < 4)
                def _():
                    pl.semaphore_signal(
                        go, inc=1, device_id={"row": r + 1}, device_id_type=MESH
                    )

            if hop == 1:
                take_rows()
        solve(0)

    def ring_kind(hop, below):
        for direction, quarter in ORDER:
            if hop < hops(direction, quarter):
                @pl.when((shard_of(direction, hop + 1) < 4) == below)
                def _():
                    ring_step(direction, quarter, hop)

    @pl.when(r == 1)
    def _():
        @pl.when(later)
        def _():
            pl.semaphore_wait(go, 1)
            ring_begin()

        for hop in range(5):
            if hop < 4:
                ring_kind(hop, False)
            if hop >= 1:
                ring_kind(hop - 1, True)
            if hop == 2:
                take_rows()

        for b in range(4):
            block_copy(b).wait_recv()
            pivoted[...] = pivoted[...] - dot3(
                gathered[b], solved[b * PIECE : (b + 1) * PIECE]
            )
        solve(1)

    @pl.when(r >= 2)
    def _():
        ring_hop(0, 0)
        ring_hop(0, 1)
        take_rows()
        ring_hop(1, 0)
        spread(0)
        ring_hop(1, 1)
        spread(1)
        pair(0)
        ring_hop(2, 0)
        pair(1)
        spread(2)
        ring_hop(2, 1)
        spread(3)
        pair(2)
        ring_hop(3, 0)
        ring_hop(3, 1)

        def early(group, _):
            pair_copy(group).wait_recv()
            update(group)
            return 0

        lax.fori_loop(0, 2, early, 0)
        for k in range(2):
            for b in range(2):
                columns = slice(b * PIECE, (b + 1) * PIECE)
                high, low = halves(gathered[4 + 2 * k + b])
                tile_high[k, :, columns] = high
                tile_low[k, :, columns] = low

        def product(k):
            high, low = halves(solved[(2 + k) * HALF : (3 + k) * HALF])
            small = jnp.dot(tile_high[k], low, preferred_element_type=F32)
            small = small + jnp.dot(tile_low[k], high, preferred_element_type=F32)
            return small + jnp.dot(tile_high[k], high, preferred_element_type=F32)

        pair(3)
        pair_copy(2).wait_recv()
        pivoted[...] = pivoted[...] - product(0)
        pair_copy(3).wait_recv()
        out_ref[...] = pivoted[...] - product(1)
        for group in range(4):
            passed(group)

    rows_done.wait_send()
    for hop in range(4):
        for direction, quarter in ORDER:
            if hop < hops(direction, quarter):
                ring_sent(direction, quarter, hop)


def body(objective, pivots, panel):
    width = objective.shape[1]
    dma = pltpu.SemaphoreType.DMA
    vmem = pl.BlockSpec(memory_space=pltpu.VMEM)
    arrays = [
        pltpu.with_memory_space_constraint(array, pltpu.HBM)
        for array in (objective, pivots.reshape(1, NB), panel)
    ]
    return pl.pallas_call(
        kernel,
        out_shape=jax.ShapeDtypeStruct(objective.shape, F32),
        in_specs=[pl.BlockSpec(memory_space=pl.ANY)] * 3,
        out_specs=vmem,
        scratch_shapes=[
            pltpu.VMEM(objective.shape, F32), pltpu.VMEM((1, NB), jnp.int32), dma, dma, dma,
            pltpu.SemaphoreType.REGULAR,
            pltpu.VMEM((2, NB, HALF), BF16), pltpu.VMEM((2, NB, HALF), BF16),
            pltpu.VMEM((COLS, NB, PIECE), F32),
            pltpu.VMEM((HALF, width), F32),
            pltpu.VMEM((HALF, width), F32),
            pltpu.VMEM((2 * NB, width), F32),
            pltpu.VMEM((NB, width), F32),
            dma, dma,
            dma((2, 4, 4)), dma((2, 4, 4)),
            dma((4,)), dma((4,)), dma((4,)), dma((4,)), dma((4,)), dma((4,)), dma((4,)), dma((4,)),
        ],
        compiler_params=pltpu.CompilerParams(
            collective_id=0, has_side_effects=True, vmem_limit_bytes=48 * 1024 * 1024
        ),
        name="zonal",
    )(*arrays)


def solution(mesh):
    in_specs = (P("row", "col"), P("row"), P("row", "col"))
    out_specs = P("row", "col")
    return jax.shard_map(body, mesh=mesh, in_specs=in_specs, out_specs=out_specs, check_vma=False)
```
